32 devices in a mesh: band: 8 (over z, y), lon: 4 (over x, core).
Axes of the slice: x: 2, y: 2, z: 4, core: 2. Of those that a mesh axis runs over, the one named last changes fastest.
Arguments:
- state: bfloat16 [822, 16, 2048], P(None, 'band', 'lon'), may hold values from -6 to 6
- kernel: float32 [822, 3, 3], replicated, may hold values from -6 to 6
- w_state: bfloat16 [256, 822], replicated, may hold values from -0.21875 to 0.21875
- w_conv: bfloat16 [256, 822], replicated, may hold values from -0.21875 to 0.21875
- w_adj: bfloat16 [256, 822], replicated, may hold values from -0.875 to 0.875
- bias_in: float32 [256], replicated, may hold values from -6 to 6
- w_out: bfloat16 [822, 256], replicated, may hold values from -0.375 to 0.375
- obs_op: bfloat16 [96, 822], replicated, may hold values from -0.078125 to 0.078125
- observations: float32 [96, 8, 512], P(None, 'band', 'lon'), may hold values from -12 to 12
- obs_mask: int32 [96, 8, 512], P(None, 'band', 'lon'), may hold values 0 or 1
- dual_in: bfloat16 [96, 8, 512], P(None, 'band', 'lon'), may hold values from -6 to 6
- dual_res: bfloat16 [256, 96], replicated, may hold values from -0.625 to 0.625
- dual_prev: bfloat16 [256, 96], replicated, may hold values from -0.625 to 0.625
- dual_bias: float32 [256], replicated, may hold values from -6 to 6
- dual_out_w: bfloat16 [96, 256], replicated, may hold values from -0.375 to 0.375
- footprint: int32 [8, 4, 8, 4], P('band', 'lon'), may hold values from 0 to 7, all different within a row; in each aligned block of 8 rows (0 to 7, 8 to 15, ..., all dimensions but the last counted through in order) at most 8 rows name the same one
Outputs:
- state_out: bfloat16 [822, 16, 2048], P(None, 'band', 'lon')
- dual_out: bfloat16 [96, 8, 512], P(None, 'band', 'lon')
The draws below stay inside these ranges and needn't reach their ends.
Inputs may be any that keep to these rules, and one draw needn't show every extreme that they name: `footprint`: within the 8 column blocks of one pair (b, l), the 4 entries of a block differ, and no value appears more than 8 times; in some pairs one value appears exactly 8 times.
All inputs are finite; a program needn't handle non-finite values. No bound on the sum of `obs_mask` on one device may be relied on, other than what follows from the above.
Results may differ from the reference program's by a relative error of at most 0.0075.
Values may be sent and summed in bfloat16 or wider, within the bound.
A program may use at most 64 MiB of HBM per device.

```python
import math
import jax
import jax.numpy as jnp
import numpy as np
from jax import lax

CH = 822
HID = 256
RADCH = 96
DHID = 256
PIX = 128
TOP = 4
LAT_DEV = 2
OWNERS = 8
NCBL = 4
CB_DEV = 8
MOST = 8
NLAT = 16
NLON = 2048
N_BAND = 8
N_LON = 4


def touch_ends(drawn, rng, smallest, top_value):
    extent = drawn.shape
    spot = [jax.random.randint(jax.random.fold_in(rng, axis), (), 0, extent[axis]) for axis in range(len(extent))]
    drawn = drawn.at[tuple(spot)].set(smallest)
    longest = extent.index(max(extent))
    spot[longest] = (spot[longest] + 1) % extent[longest]
    return drawn.at[tuple(spot)].set(top_value)


def block_scale(own_key, extent, split, low, top_value):
    level = 1.0
    for axis_at, blocks in split:
        heights = jax.random.uniform(jax.random.fold_in(jax.random.fold_in(own_key, 6), axis_at), (blocks,), jnp.float32, low / len(split), top_value / len(split))
        level = level * jnp.repeat(jnp.exp(heights), extent[axis_at] // blocks).reshape((-1,) + (1,) * (len(extent) - 1 - axis_at))
    return level


def routed_block(key, own, number, rows, count, top, reach, lean):
    sequence = jax.random.permutation(key, count)
    heavy_load, ordinary = portions_of(count, rows * top, reach, lean, True), portions_of(count, rows * top, reach, lean, False)
    places = jnp.arange(count)

    def named(tallies, offset_by):
        used = int((tallies > 0).sum())
        fixed = max(1, used // 4)
        passed = fixed + (places - fixed + offset_by * (used - fixed)) % max(1, count - fixed)
        return jnp.zeros((count,), jnp.int32).at[sequence[jnp.where(places < fixed, places, passed)]].set(jnp.asarray(tallies, jnp.int32))

    tallies = jnp.where(number % 4 == 0, named(heavy_load, number // 4), named(ordinary, number - number // 4 - 1))
    mixed = jax.random.permutation(jax.random.fold_in(own, 3), count)
    source_of, receiver = mixed[0:count // 2 * 2:2], mixed[1:count // 2 * 2:2]
    room = jnp.minimum(tallies[source_of] - 1, reach - tallies[receiver]) // 2
    room = jnp.where((source_of == sequence[0]) | (receiver == sequence[0]) | (tallies[receiver] == 0), 0, jnp.maximum(room, 0))
    passed = jax.random.randint(jax.random.fold_in(own, 4), (count // 2,), 0, 1 << 20) % (room + 1)
    tallies = tallies.at[source_of].add(-passed).at[receiver].add(passed)
    items = jnp.searchsorted(jnp.cumsum(tallies), jnp.arange(rows * top), side="right").astype(jnp.int32)
    table = items.reshape(top, rows).T
    table = table[jax.random.permutation(jax.random.fold_in(own, 1), rows)]
    offset_by = jax.random.randint(jax.random.fold_in(own, 2), (rows, 1), 0, top)
    return jnp.take_along_axis(table, (jnp.arange(top)[None, :] + offset_by) % top, axis=1)


def portions_of(number_of, total, most, lean, full):
    loads = [(1 << 20) // math.isqrt(standing ** lean) + 1 for standing in range(1, number_of + 1)]
    largest = most if full else min(most, max(-(-total // number_of), total * loads[0] // sum(loads)))
    least = 1 if total - largest >= number_of - 1 else 0
    counts, surplus = [largest] + [least] * (number_of - 1), total - largest - least * (number_of - 1)
    while surplus > 0:
        candidates = [i for i in range(1, number_of) if counts[i] < largest] or [i for i in range(1, number_of) if counts[i] < most]
        mass, remaining = sum([loads[i] for i in candidates]), surplus
        for i in candidates:
            more = min(most - counts[i], max(1, remaining * loads[i] // mass), surplus)
            counts[i] = counts[i] + more
            surplus = surplus - more
    return np.array(counts)


def noise(key, shape, scale, most, pieces=(), kind=jnp.bfloat16):
    values = jax.random.normal(key, shape, jnp.float32) * scale
    if len(pieces) > 0:
        values = block_scale(key, shape, pieces, -0.22, 0.18) * values
    return jnp.clip(values, min=-most, max=most).astype(kind)


def setup_inputs(seed: int = 0) -> dict:
    key_of = jax.random.split(jax.random.key(seed), 17)
    state = noise(key_of[0], (CH, NLAT, NLON), 1.0, 6.0, ((1, 8), (2, 4)))
    kernel = noise(key_of[1], (CH, 3, 3), 0.4, 6.0, (), jnp.float32)
    w_state = noise(key_of[2], (HID, CH), CH ** -0.5, 0.21875)
    w_conv = noise(key_of[3], (HID, CH), CH ** -0.5, 0.21875)
    w_adj = noise(key_of[4], (HID, CH), (CH // 16) ** -0.5, 0.875)
    bias_in = noise(key_of[5], (HID,), 1.0, 6.0, (), jnp.float32)
    w_out = noise(key_of[6], (CH, HID), HID ** -0.5, 0.375)
    obs_op = noise(key_of[7], (RADCH, CH), (CH * CB_DEV * TOP // 4) ** -0.5, 0.078125)
    observations = noise(key_of[8], (RADCH, OWNERS, NLON // NCBL), 2.0, 12.0, ((1, 8), (2, 4)), jnp.float32)
    obs_mask = touch_ends((jax.random.randint(key_of[9], (RADCH, OWNERS, NLON // NCBL), 0, 4) < 3).astype(jnp.int32), jax.random.fold_in(key_of[9], 1), 0, 1)
    dual_in = noise(key_of[10], (RADCH, OWNERS, NLON // NCBL), 1.0, 6.0, ((1, 8), (2, 4)))
    dual_res = noise(key_of[11], (DHID, RADCH), RADCH ** -0.5, 0.625)
    dual_prev = noise(key_of[12], (DHID, RADCH), RADCH ** -0.5, 0.625)
    dual_bias = noise(key_of[13], (DHID,), 1.0, 6.0, (), jnp.float32)
    dual_out_w = noise(key_of[14], (RADCH, DHID), DHID ** -0.5, 0.375)
    footprint_keys = jax.random.split(jax.random.fold_in(key_of[15], 1), N_BAND * N_LON * CB_DEV // CB_DEV)
    footprint_turns = jax.random.permutation(jax.random.fold_in(key_of[15], 3), N_BAND * N_LON * CB_DEV // CB_DEV)
    footprint = jax.vmap(lambda own, number: routed_block(jax.random.fold_in(key_of[15], 2), own, number, CB_DEV, OWNERS, TOP, MOST, 2))(footprint_keys, footprint_turns).reshape((N_BAND, N_LON, CB_DEV, TOP))
    return dict(state=state, kernel=kernel, w_state=w_state, w_conv=w_conv, w_adj=w_adj, bias_in=bias_in, w_out=w_out, obs_op=obs_op, observations=observations, obs_mask=obs_mask, dual_in=dual_in, dual_res=dual_res, dual_prev=dual_prev, dual_bias=dual_bias, dual_out_w=dual_out_w, footprint=footprint)


def reference(state, kernel, w_state, w_conv, w_adj, bias_in, w_out, obs_op, observations, obs_mask, dual_in, dual_res, dual_prev, dual_bias, dual_out_w, footprint):
    cover = jnp.sum((footprint[..., None] == jnp.arange(OWNERS, dtype=jnp.int32)).astype(jnp.float32), axis=3)
    operator32 = obs_op.astype(jnp.float32)
    bands = jnp.arange(N_BAND, dtype=jnp.int32)

    def forward(total, index):
        rows = lax.dynamic_slice_in_dim(state, (index * LAT_DEV).astype(jnp.int32), LAT_DEV, 1)
        cols = rows.reshape(CH, LAT_DEV, N_LON, NCBL, PIX).astype(jnp.float32)
        proj = jnp.einsum('rc,cilmp->limrp', operator32, cols).astype(jnp.bfloat16)
        proj = proj.reshape(N_LON, CB_DEV, RADCH, PIX).astype(jnp.float32)
        share = jnp.einsum('lkd,lkrp->rdlp', cover[index], proj).astype(jnp.bfloat16)
        share = lax.optimization_barrier(share)
        total = total + share.astype(jnp.float32)
        return total, None

    start = jnp.zeros((RADCH, OWNERS, N_LON, PIX), jnp.float32)
    evolved, unused = lax.scan(forward, start, bands)
    evolved = evolved.reshape(RADCH, OWNERS, N_LON * PIX)
    departure = jnp.where(obs_mask == 1, evolved - observations, 0.0).astype(jnp.bfloat16)
    pre = jnp.einsum('hr,rbn->hbn', dual_res.astype(jnp.float32), departure.astype(jnp.float32))
    pre = pre + jnp.einsum('hr,rbn->hbn', dual_prev.astype(jnp.float32), dual_in.astype(jnp.float32))
    dual_hidden = jax.nn.gelu(pre + dual_bias[:, None, None]).astype(jnp.bfloat16)
    dual_out = (dual_in.astype(jnp.float32) + jnp.einsum('rh,hbn->rbn', dual_out_w.astype(jnp.float32), dual_hidden.astype(jnp.float32))).astype(jnp.bfloat16)
    lam = dual_out.reshape(RADCH, OWNERS, N_LON, PIX).astype(jnp.float32)
    wrapped = jnp.concatenate([state[:, :, -1:], state, state[:, :, :1]], axis=2)
    padded = jnp.pad(wrapped, ((0, 0), (1, 1), (0, 0)))

    def primal(index):
        back = jnp.einsum('lkd,rdlp->lkrp', cover[index], lam).astype(jnp.bfloat16)
        adj = jnp.einsum('rc,lkrp->clkp', operator32, back.astype(jnp.float32)).astype(jnp.bfloat16)
        adj = adj.reshape(CH, N_LON, LAT_DEV, NCBL, PIX).transpose(0, 2, 1, 3, 4).reshape(CH, LAT_DEV * NLON)
        window = lax.dynamic_slice(padded, (jnp.int32(0), (index * LAT_DEV).astype(jnp.int32), jnp.int32(0)), (CH, LAT_DEV + 2, NLON + 2))
        conv = jnp.zeros((CH, LAT_DEV, NLON), jnp.float32)
        for a in range(3):
            for e in range(3):
                conv = conv + kernel[:, a, e][:, None, None] * window[:, a:a + LAT_DEV, e:e + NLON].astype(jnp.float32)
        conv = conv.astype(jnp.bfloat16).reshape(CH, LAT_DEV * NLON)
        rows = lax.dynamic_slice_in_dim(state, (index * LAT_DEV).astype(jnp.int32), LAT_DEV, 1).reshape(CH, LAT_DEV * NLON)
        pre_state = jnp.dot(w_state, rows, preferred_element_type=jnp.float32)
        pre_state = pre_state + jnp.dot(w_conv, conv, preferred_element_type=jnp.float32)
        pre_state = pre_state + jnp.dot(w_adj, adj, preferred_element_type=jnp.float32)
        hidden = jax.nn.gelu(pre_state + bias_in[:, None]).astype(jnp.bfloat16)
        result = rows.astype(jnp.float32) + jnp.dot(w_out, hidden, preferred_element_type=jnp.float32)
        return result.astype(jnp.bfloat16).reshape(CH, LAT_DEV, NLON)

    stacked = lax.map(primal, bands)
    state_out = stacked.transpose(1, 0, 2, 3).reshape(CH, NLAT, NLON)
    return state_out, dual_out
```

```python
import jax
import jax.numpy as jnp
from jax import lax
from jax.sharding import PartitionSpec as P

PIX = 128
TOP = 4


def extended(value, sides, width, wrap):
    for axis, dim in sides:
        count, length = (lax.axis_size(axis), value.shape[dim])
        up = [(i, (i + 1) % count) for i in range(count if wrap else count - 1)]
        down = [(j, i) for i, j in up]
        last = lax.slice_in_dim(value, length - width, length, axis=dim)
        initial = lax.slice_in_dim(value, 0, width, axis=dim)
        before = lax.ppermute(last, axis, up)
        after = lax.ppermute(initial, axis, down)
        value = jnp.concatenate([before, value, after], axis=dim)
    return value


def on_device(
    state,
    kernel,
    w_state,
    w_conv,
    w_adj,
    bias_in,
    w_out,
    obs_op,
    observations,
    obs_mask,
    dual_in,
    dual_res,
    dual_prev,
    dual_bias,
    dual_out_w,
    footprint,
):
    channels, lat_rows, lon_cols = state.shape
    radiance = obs_op.shape[0]
    owners = lax.axis_size("band")
    nblocks = lat_rows * lon_cols // PIX
    routes = footprint.reshape(nblocks, TOP)
    targets = jnp.arange(owners, dtype=jnp.int32)
    member = (routes[:, :, None] == targets[None, None, :]).astype(jnp.int32)
    cover = jnp.sum(member, axis=1).astype(jnp.bfloat16)
    columns = state.reshape(channels, nblocks, PIX)
    projected = jnp.einsum(
        "rc,ckp->krp", obs_op, columns, preferred_element_type=jnp.float32
    ).astype(jnp.bfloat16)
    partial_sums = jnp.einsum(
        "kd,krp->drp", cover, projected, preferred_element_type=jnp.float32
    ).astype(jnp.bfloat16)
    widened = extended(state, (("lon", 2),), 1, True).astype(jnp.float32)

    def taps(a, row):
        total = jnp.zeros((channels, lon_cols), jnp.float32)
        for e in range(3):
            total = total + kernel[:, a, e][:, None] * widened[:, row, e : e + lon_cols]
        return total

    def mixed(value):
        return jnp.dot(w_conv, value.astype(jnp.bfloat16), preferred_element_type=jnp.float32)

    bands = lax.axis_size("band")
    to_next = [(i, i + 1) for i in range(bands - 1)]
    to_previous = [(i + 1, i) for i in range(bands - 1)]
    from_above = lax.ppermute(mixed(taps(0, lat_rows - 1)).astype(jnp.bfloat16), "band", to_next)
    from_below = lax.ppermute(mixed(taps(2, 0)).astype(jnp.bfloat16), "band", to_previous)
    rows = []
    for i in range(lat_rows):
        own = sum(taps(a, i + a - 1) for a in range(3) if 0 <= i + a - 1 < lat_rows)
        part = mixed(own)
        part = part + jnp.dot(w_state, state[:, i], preferred_element_type=jnp.float32)
        if i == 0:
            part = part + from_above.astype(jnp.float32)
        if i == lat_rows - 1:
            part = part + from_below.astype(jnp.float32)
        rows.append(part)
    pre_state = jnp.concatenate(rows, axis=1)
    flat_state = state.reshape(channels, lat_rows * lon_cols)
    through = lax.dot_general(
        w_adj, obs_op, (((1,), (1,)), ((), ())), preferred_element_type=jnp.float32
    ).astype(jnp.bfloat16)
    arrived = lax.all_to_all(partial_sums, "band", split_axis=0, concat_axis=0, tiled=True)
    evolved = jnp.sum(arrived, axis=0, dtype=jnp.float32)
    observed = observations.reshape(radiance, PIX)
    valid = obs_mask.reshape(radiance, PIX)
    dual_now = dual_in.reshape(radiance, PIX)
    departure = jnp.where(valid == 1, evolved - observed, 0.0).astype(jnp.bfloat16)
    pre_dual = jnp.dot(dual_res, departure, preferred_element_type=jnp.float32)
    pre_dual = pre_dual + jnp.dot(dual_prev, dual_now, preferred_element_type=jnp.float32)
    dual_hidden = jax.nn.gelu(pre_dual + dual_bias[:, None]).astype(jnp.bfloat16)
    dual_new = (
        dual_now.astype(jnp.float32)
        + jnp.dot(dual_out_w, dual_hidden, preferred_element_type=jnp.float32)
    ).astype(jnp.bfloat16)
    spread = jnp.broadcast_to(dual_new[None], (owners,) + dual_new.shape)
    everyone = lax.all_to_all(spread, "band", split_axis=0, concat_axis=0, tiled=True)
    back_sum = jnp.einsum("kd,drp->rkp", cover, everyone, preferred_element_type=jnp.float32)
    back = back_sum.astype(jnp.bfloat16).reshape(radiance, nblocks * PIX)
    pre_state = pre_state + jnp.dot(through, back, preferred_element_type=jnp.float32)
    hidden = jax.nn.gelu(pre_state + bias_in[:, None]).astype(jnp.bfloat16)
    updated = flat_state.astype(jnp.float32) + jnp.dot(
        w_out, hidden, preferred_element_type=jnp.float32
    )
    state_out = updated.astype(jnp.bfloat16).reshape(channels, lat_rows, lon_cols)
    return (state_out, dual_new.reshape(radiance, 1, PIX))


def solution(mesh):
    in_specs = (
        P(None, "band", "lon"),
        P(),
        P(),
        P(),
        P(),
        P(),
        P(),
        P(),
        P(None, "band", "lon"),
        P(None, "band", "lon"),
        P(None, "band", "lon"),
        P(),
        P(),
        P(),
        P(),
        P("band", "lon", None, None),
    )
    out_specs = (P(None, "band", "lon"), P(None, "band", "lon"))
    return jax.shard_map(
        on_device, mesh=mesh, in_specs=in_specs, out_specs=out_specs, check_vma=False
    )
```

```python
import jax
import jax.numpy as jnp
import numpy as np
from jax import lax
from jax.experimental import pallas as pl
from jax.experimental.pallas import tpu as pltpu
from jax.sharding import PartitionSpec as P

PIX = 128
MESH = pl.DeviceIdType.MESH
STEP = 32
SLOTS = 16
EDGES = tuple((db, dl) for db in (0, -1, 1) for dl in (-1, 1))


def dot(a, b, da=1, db=0):
    return lax.dot_general(a, b, (((da,), (db,)), ((), ())), preferred_element_type=jnp.float32)


def picker(lat_rows):
    pick = np.zeros((len(EDGES) * SLOTS, lat_rows * 2 * PIX), np.float32)
    for m, (db, dl) in enumerate(EDGES):
        for i in range(lat_rows):
            relative = i - lat_rows * db
            if -1 <= relative <= lat_rows:
                if dl == -1:
                    pick[m * SLOTS + relative + 1, i * 2 * PIX] = 1.0
                else:
                    pick[m * SLOTS + lat_rows + 2 + relative + 1, i * 2 * PIX + 2 * PIX - 1] = 1.0
    return pick


def kernel_body(
    state,
    taps,
    edge0,
    edge1,
    ws_t,
    wc_t,
    wa_t,
    bias,
    w_out,
    obs_op,
    observed,
    valid,
    dual_in,
    res_t,
    prev_t,
    dual_bias,
    dual_out_w,
    cover,
    pick,
    out,
    dual_new,
    xb,
    wide,
    rows,
    mix,
    pre,
    zbuf,
    share,
    arrived,
    gathered,
    back,
    through_t,
    hid,
    psend,
    precv,
    esend,
    erecv,
    load_sem,
    a_send,
    a_recv,
    g_send,
    g_recv,
    p_send,
    p_recv,
    e_send,
    e_recv,
):
    channels = ws_t.shape[0]
    lon_cols = xb.shape[1]
    per_row = lon_cols // PIX
    radiance = obs_op.shape[0]
    nb = lax.axis_size("band")
    nl = lax.axis_size("lon")
    nblocks = 2 * per_row
    b = lax.axis_index("band")
    l = lax.axis_index("lon")
    flat = state.reshape(2 * channels, lon_cols)
    load = pltpu.make_async_copy(flat, xb, load_sem.at[0])
    load.start()

    precv[...] = jnp.zeros_like(precv)
    erecv[...] = jnp.zeros_like(erecv)
    barrier = pltpu.get_barrier_semaphore()

    def greet(off, carry):
        pl.semaphore_signal(
            barrier, inc=1, device_id=(lax.rem(b + off, nb), l), device_id_type=MESH
        )
        return carry

    lax.fori_loop(1, nb, greet, 0)
    for db, dl in EDGES:

        @pl.when((b + db >= 0) & (b + db < nb))
        def _():
            pl.semaphore_signal(
                barrier, inc=1, device_id=(b + db, lax.rem(l + dl + nl, nl)), device_id_type=MESH
            )

    through_t[...] = dot(obs_op[...], wa_t[...]).astype(jnp.bfloat16)
    load.wait()

    whole = channels // STEP * STEP

    def chunks(body):
        def step(i, carry):
            body(pl.multiple_of(i * STEP, STEP), STEP)
            return carry

        lax.fori_loop(0, whole // STEP, step, 0)
        if channels > whole:
            body(whole, channels - whole)

    def split(c0, n):
        both = xb[pl.ds(2 * c0, 2 * n), :].astype(jnp.float32)
        for q in range(per_row):
            wide[q, pl.ds(2 * c0, 2 * n), :] = both[:, q * PIX : (q + 1) * PIX]
        for i in range(2):
            for q in range(per_row):
                rows[i, pl.ds(c0, n), q * PIX : (q + 1) * PIX] = wide[
                    q, pl.ds(2 * c0 + i, n, 2), :
                ].astype(jnp.bfloat16)

    chunks(split)
    for i in range(2):
        zbuf[:, i * lon_cols : (i + 1) * lon_cols] = dot(obs_op[...], rows[i]).astype(jnp.bfloat16)

    pl.semaphore_wait(
        barrier,
        nb - 1 + 2 + 2 * (b > 0).astype(jnp.int32) + 2 * (b < nb - 1).astype(jnp.int32),
    )

    def to_owner(off):
        d = lax.rem(b + off, nb)
        return pltpu.make_async_remote_copy(
            src_ref=share.at[d],
            dst_ref=arrived.at[off],
            send_sem=a_send.at[off],
            recv_sem=a_recv.at[off],
            device_id=(d, l),
            device_id_type=MESH,
        )

    def make_share(off):
        d = lax.rem(b + off, nb)
        total = jnp.zeros((radiance, PIX), jnp.float32)
        for k in range(nblocks):
            total = total + cover[k, d] * zbuf[:, k * PIX : (k + 1) * PIX].astype(jnp.float32)
        share[d] = total.astype(jnp.bfloat16)

    def send_share(off, carry):
        make_share(off)
        to_owner(off).start()
        return carry

    lax.fori_loop(1, nb, send_share, 0)
    make_share(0)

    lane = lax.broadcasted_iota(jnp.int32, (1, lon_cols), 1)

    def taps_of(targets):
        def body(c0, n):
            x = [rows[i, pl.ds(c0, n), :].astype(jnp.float32) for i in range(2)]
            tap = taps[pl.ds(c0, n), :]
            for t in targets:
                parts = []
                for e in range(3):
                    total = None
                    for i in range(2):
                        a = i - (t - 1) + 1
                        if 0 <= a < 3:
                            term = tap[:, 3 * a + e : 3 * a + e + 1] * x[i]
                            total = term if total is None else total + term
                    parts.append(total)
                west = jnp.where(lane == 0, 0.0, pltpu.roll(parts[0], 1, 1))
                east = jnp.where(lane == lon_cols - 1, 0.0, pltpu.roll(parts[2], lon_cols - 1, 1))
                mix[t, pl.ds(c0, n), :] = (parts[1] + west + east).astype(jnp.bfloat16)

        return body

    chunks(taps_of((0, 3)))

    def to_neighbour(which):
        return pltpu.make_async_remote_copy(
            src_ref=psend.at[which],
            dst_ref=precv.at[which],
            send_sem=p_send.at[which],
            recv_sem=p_recv.at[which],
            device_id=(b - 1 if which == 0 else b + 1, l),
            device_id_type=MESH,
        )

    reaches = (b > 0, b < nb - 1)
    for which in range(2):
        psend[which] = dot(wc_t[...], mix[3 * which], 0, 0).astype(jnp.bfloat16)

        @pl.when(reaches[which])
        def _():
            to_neighbour(which).start()

    elane = lax.broadcasted_iota(jnp.int32, (1, PIX), 1)
    ends = []
    for i in range(2):
        initial = rows[i, :, 0:PIX].astype(jnp.float32)[:, 0:1]
        last = rows[i, :, lon_cols - PIX : lon_cols].astype(jnp.float32)[:, PIX - 1 : PIX]
        ends.append(jnp.where(elane < 4, last, initial))
    edge = (ends[0] * edge0[...] + ends[1] * edge1[...]).astype(jnp.bfloat16)
    esend[...] = dot(edge, wc_t[...], 0, 0)[0:SLOTS].astype(jnp.bfloat16)

    def to_edge(m):
        db, dl = EDGES[m]
        return pltpu.make_async_remote_copy(
            src_ref=esend,
            dst_ref=erecv.at[pl.ds(m * SLOTS, SLOTS)],
            send_sem=e_send.at[m],
            recv_sem=e_recv.at[m],
            device_id=(b - db, lax.rem(l - dl + nl, nl)),
            device_id_type=MESH,
        )

    for m, (db, dl) in enumerate(EDGES):

        @pl.when((b - db >= 0) & (b - db < nb))
        def _():
            to_edge(m).start()

    def take_share(off, total):
        to_owner(off).wait_recv()
        return total + arrived[off].astype(jnp.float32)

    evolved = lax.fori_loop(1, nb, take_share, share[b].astype(jnp.float32))
    departure = jnp.where(valid[...] == 1, evolved - observed[...], 0.0).astype(jnp.bfloat16)
    pre_dual = dot(res_t[...], departure, 0, 0) + dot(prev_t[...], dual_in[...], 0, 0)
    dual_hidden = jax.nn.gelu(pre_dual + dual_bias[...]).astype(jnp.bfloat16)
    updated = dual_in[...].astype(jnp.float32) + dot(dual_out_w[...], dual_hidden)
    gathered[0] = updated.astype(jnp.bfloat16)
    dual_new[...] = updated.astype(jnp.bfloat16)

    def to_all(off):
        return pltpu.make_async_remote_copy(
            src_ref=gathered.at[0],
            dst_ref=gathered.at[off],
            send_sem=g_send.at[off],
            recv_sem=g_recv.at[off],
            device_id=(lax.rem(b + off, nb), l),
            device_id_type=MESH,
        )

    def send_dual(off, carry):
        to_all(off).start()
        return carry

    lax.fori_loop(1, nb, send_dual, 0)

    chunks(taps_of((1, 2)))
    for i in range(2):
        pre[i] = dot(ws_t[...], rows[i], 0, 0) + dot(wc_t[...], mix[1 + i], 0, 0) + bias[...]

    def landed(off, carry):
        to_all(off).wait_recv()
        return carry

    lax.fori_loop(1, nb, landed, 0)
    for r in range(0, radiance, 16):

        def gather_in(off, totals):
            d = lax.rem(b - off + nb, nb)
            block = gathered[off, r : r + 16, :].astype(jnp.float32)
            return tuple(totals[k] + cover[k, d] * block for k in range(nblocks))

        zero = jnp.zeros((16, PIX), jnp.float32)
        totals = lax.fori_loop(0, nb, gather_in, (zero,) * nblocks, unroll=nb <= 8)
        for k in range(nblocks):
            back[r : r + 16, k * PIX : (k + 1) * PIX] = totals[k].astype(jnp.bfloat16)

    for m, (db, dl) in enumerate(EDGES):

        @pl.when((b + db >= 0) & (b + db < nb))
        def _():
            to_edge(m).wait_recv()

    fix = dot(erecv[...], pick[...], 0, 0)
    for i in range(2):
        pre[i] = pre[i] + dot(
            through_t[...], back[:, i * lon_cols : (i + 1) * lon_cols], 0, 0
        )
        pre[i, :, 0:PIX] = pre[i, :, 0:PIX] + fix[:, 2 * i * PIX : (2 * i + 1) * PIX]
        pre[i, :, lon_cols - PIX :] = (
            pre[i, :, lon_cols - PIX :] + fix[:, (2 * i + 1) * PIX : (2 * i + 2) * PIX]
        )
    for i in range(2):
        came = 1 - i

        @pl.when(reaches[i])
        def _():
            to_neighbour(came).wait_recv()

        for q in range(per_row):
            cols = slice(q * PIX, (q + 1) * PIX)
            hid[:, cols] = jax.nn.gelu(
                pre[i, :, cols] + precv[came, :, cols].astype(jnp.float32)
            ).astype(jnp.bfloat16)
        for q in range(per_row):
            cols = slice(q * PIX, (q + 1) * PIX)
            place = pl.ds(i, channels, 2)
            wide[q, place, :] = wide[q, place, :] + dot(w_out[...], hid[:, cols])

    def pack(c0, n):
        for q in range(per_row):
            xb[pl.ds(2 * c0, 2 * n), q * PIX : (q + 1) * PIX] = wide[
                q, pl.ds(2 * c0, 2 * n), :
            ].astype(jnp.bfloat16)

    chunks(pack)
    store = pltpu.make_async_copy(xb, out.reshape(2 * channels, lon_cols), load_sem.at[0])
    store.start()

    def sent(off, carry):
        to_owner(off).wait_send()
        to_all(off).wait_send()
        return carry

    lax.fori_loop(1, nb, sent, 0)
    for which in range(2):

        @pl.when(reaches[which])
        def _():
            to_neighbour(which).wait_send()

    for m, (db, dl) in enumerate(EDGES):

        @pl.when((b - db >= 0) & (b - db < nb))
        def _():
            to_edge(m).wait_send()

    store.wait()


def on_device(
    state,
    kernel,
    w_state,
    w_conv,
    w_adj,
    bias_in,
    w_out,
    obs_op,
    observations,
    obs_mask,
    dual_in,
    dual_res,
    dual_prev,
    dual_bias,
    dual_out_w,
    footprint,
):
    channels, lat_rows, lon_cols = state.shape
    assert lat_rows == 2
    radiance = obs_op.shape[0]
    hidden = w_state.shape[0]
    nb = lax.axis_size("band")
    nblocks = lat_rows * lon_cols // PIX
    routes = footprint.reshape(nblocks, footprint.shape[-1])
    targets = jnp.arange(nb, dtype=jnp.int32)
    member = (routes[:, :, None] == targets[None, None, :]).astype(jnp.float32)
    cover = jnp.sum(member, axis=1)
    taps = kernel.reshape(channels, 9)
    none = jnp.zeros((channels,), jnp.float32)
    west, east = ([kernel[:, a, e] for a in range(3)] for e in (0, 2))
    on0 = [west[2], west[1], west[0], none, east[2], east[1], east[0], none]
    on1 = [none, west[2], west[1], west[0], none, east[2], east[1], east[0]]
    edge0, edge1 = (
        jnp.pad(jnp.stack(cols, axis=1), ((0, 0), (0, PIX - len(cols)))) for cols in (on0, on1)
    )
    pick = jnp.asarray(picker(lat_rows), jnp.bfloat16)
    vmem = pl.BlockSpec(memory_space=pltpu.VMEM)
    anywhere = pl.BlockSpec(memory_space=pl.ANY)
    smem = pl.BlockSpec(memory_space=pltpu.SMEM)
    dma = pltpu.SemaphoreType.DMA
    bf16, f32 = jnp.bfloat16, jnp.float32
    state_out, dual_new = pl.pallas_call(
        kernel_body,
        out_shape=(
            jax.ShapeDtypeStruct(state.shape, bf16),
            jax.ShapeDtypeStruct((radiance, PIX), bf16),
        ),
        in_specs=[anywhere] + [vmem] * 16 + [smem, vmem],
        out_specs=(anywhere, vmem),
        scratch_shapes=[
            pltpu.VMEM((2 * channels, lon_cols), bf16),
            pltpu.VMEM((lon_cols // PIX, 2 * channels, PIX), f32),
            pltpu.VMEM((2, channels, lon_cols), bf16),
            pltpu.VMEM((4, channels, lon_cols), bf16),
            pltpu.VMEM((2, hidden, lon_cols), f32),
            pltpu.VMEM((radiance, nblocks * PIX), bf16),
            pltpu.VMEM((nb, radiance, PIX), bf16),
            pltpu.VMEM((nb, radiance, PIX), bf16),
            pltpu.VMEM((nb, radiance, PIX), bf16),
            pltpu.VMEM((radiance, nblocks * PIX), bf16),
            pltpu.VMEM((radiance, hidden), bf16),
            pltpu.VMEM((hidden, lon_cols), bf16),
            pltpu.VMEM((2, hidden, lon_cols), bf16),
            pltpu.VMEM((2, hidden, lon_cols), bf16),
            pltpu.VMEM((SLOTS, hidden), bf16),
            pltpu.VMEM((len(EDGES) * SLOTS, hidden), bf16),
            dma((1,)),
            dma((nb,)),
            dma((nb,)),
            dma((nb,)),
            dma((nb,)),
            dma((2,)),
            dma((2,)),
            dma((len(EDGES),)),
            dma((len(EDGES),)),
        ],
        compiler_params=pltpu.CompilerParams(
            collective_id=0, has_side_effects=True, vmem_limit_bytes=40 << 20
        ),
    )(
        state,
        taps,
        edge0,
        edge1,
        w_state.T,
        w_conv.T,
        w_adj.T,
        bias_in[:, None],
        w_out,
        obs_op,
        observations.reshape(radiance, PIX),
        obs_mask.reshape(radiance, PIX),
        dual_in.reshape(radiance, PIX),
        dual_res.T,
        dual_prev.T,
        dual_bias[:, None],
        dual_out_w,
        cover,
        pick,
    )
    return (state_out, dual_new.reshape(radiance, 1, PIX))


def solution(mesh):
    in_specs = (
        P(None, "band", "lon"),
        P(),
        P(),
        P(),
        P(),
        P(),
        P(),
        P(),
        P(None, "band", "lon"),
        P(None, "band", "lon"),
        P(None, "band", "lon"),
        P(),
        P(),
        P(),
        P(),
        P("band", "lon", None, None),
    )
    out_specs = (P(None, "band", "lon"), P(None, "band", "lon"))
    return jax.shard_map(
        on_device, mesh=mesh, in_specs=in_specs, out_specs=out_specs, check_vma=False
    )
```

```python
import jax
import jax.numpy as jnp
from jax import lax
from jax.experimental import pallas as pl
from jax.experimental.pallas import tpu as pltpu
from jax.sharding import PartitionSpec as P

PIX = 128
MESH = pl.DeviceIdType.MESH
STEP = 32
SLOTS = 16
EDGES = tuple((db, dl) for db in (0, -1, 1) for dl in (-1, 1))


def dot(a, b, da=1, db=0):
    return lax.dot_general(a, b, (((da,), (db,)), ((), ())), preferred_element_type=jnp.float32)


def picker(shape):
    row = lax.broadcasted_iota(jnp.int32, shape, 0)
    col = lax.broadcasted_iota(jnp.int32, shape, 1)
    pick = jnp.zeros(shape, jnp.float32)
    for m, (db, dl) in enumerate(EDGES):
        for i in range(2):
            relative = i - 2 * db
            if -1 <= relative <= 2:
                at = m * SLOTS + relative + 1 + (0 if dl == -1 else 4)
                to = i * 2 * PIX + (0 if dl == -1 else 2 * PIX - 1)
                pick = jnp.where((row == at) & (col == to), 1.0, pick)
    return pick.astype(jnp.bfloat16)


def kernel_body(
    state,
    *refs,
):
    inputs, spot, (out, dual_new), refs = refs[:14], refs[14], refs[15:17], refs[17:]
    held, refs = refs[:14], refs[14:]
    (
        kern,
        ws_t,
        wc_t,
        wa_t,
        bias,
        w_out,
        obs_op,
        observed,
        valid,
        dual_in,
        res_t,
        prev_t,
        dual_bias,
        dual_out_w,
    ) = held
    (
        cover,
        kern_rows,
        taps,
        ws,
        wc,
        xb,
        wide,
        rows,
        mix,
        pre,
        zbuf,
        share,
        arrived,
        gathered,
        back,
        through_t,
        hid,
        psend,
        precv,
        esend,
        erecv,
        load_sem,
        in_sem,
        a_send,
        a_recv,
        g_send,
        g_recv,
        p_send,
        p_recv,
        e_send,
        e_recv,
    ) = refs
    channels = ws_t.shape[0]
    lon_cols = xb.shape[1]
    per_row = lon_cols // PIX
    radiance = obs_op.shape[0]
    hidden = ws_t.shape[1]
    nb = lax.axis_size("band")
    nl = lax.axis_size("lon")
    nblocks = 2 * per_row
    b = lax.axis_index("band")
    l = lax.axis_index("lon")
    flat = state.reshape(2 * channels, lon_cols)
    load = pltpu.make_async_copy(flat, xb, load_sem.at[0])
    load.start()
    fetches = [pltpu.make_async_copy(x, y, in_sem.at[i]) for i, (x, y) in enumerate(zip(inputs, held))]
    order = (6, 0, 2, 8, 7, 9, 10, 11, 12, 13, 1, 4, 3, 5)
    for i in order:
        fetches[i].start()

    precv[...] = jnp.zeros_like(precv)
    erecv[...] = jnp.zeros_like(erecv)
    barrier = pltpu.get_barrier_semaphore()

    def greet(off, carry):
        pl.semaphore_signal(
            barrier, inc=1, device_id=(lax.rem(b + off, nb), l), device_id_type=MESH
        )
        return carry

    lax.fori_loop(1, nb, greet, 0)
    for db, dl in EDGES:

        @pl.when((b + db >= 0) & (b + db < nb))
        def _():
            pl.semaphore_signal(
                barrier, inc=1, device_id=(b + db, lax.rem(l + dl + nl, nl)), device_id_type=MESH
            )

    def covers(d, carry):
        for k in range(nblocks):
            count = jnp.int32(0)
            for t in range(spot.shape[0]):
                count = count + (spot[t, k] == d).astype(jnp.int32)
            cover[k, d] = count.astype(jnp.float32)
        return carry

    lax.fori_loop(0, nb, covers, 0)
    kern_rows[...] = jnp.zeros_like(kern_rows)
    load.wait()
    fetches[6].wait()

    whole = channels // STEP * STEP

    def chunks(body, size=STEP, unroll=1):
        def step(i, carry):
            body(pl.multiple_of(i * size, size), size)
            return carry

        lax.fori_loop(0, whole // size, step, 0, unroll=unroll)
        if channels > whole:
            body(whole, channels - whole)

    def split(c0, n):
        both = xb[pl.ds(2 * c0, 2 * n), :].astype(jnp.float32)
        for q in range(per_row):
            wide[q, pl.ds(2 * c0, 2 * n), :] = both[:, q * PIX : (q + 1) * PIX]
        for i in range(2):
            for q in range(per_row):
                rows[i, pl.ds(c0, n), q * PIX : (q + 1) * PIX] = wide[
                    q, pl.ds(2 * c0 + i, n, 2), :
                ].astype(jnp.bfloat16)

    chunks(split)
    for i in range(2):
        zbuf[:, i * lon_cols : (i + 1) * lon_cols] = dot(obs_op[...], rows[i]).astype(jnp.bfloat16)

    pl.semaphore_wait(
        barrier,
        nb - 1 + 2 + 2 * (b > 0).astype(jnp.int32) + 2 * (b < nb - 1).astype(jnp.int32),
    )

    def to_owner(off):
        d = lax.rem(b + off, nb)
        return pltpu.make_async_remote_copy(
            src_ref=share.at[d],
            dst_ref=arrived.at[off],
            send_sem=a_send.at[off],
            recv_sem=a_recv.at[off],
            device_id=(d, l),
            device_id_type=MESH,
        )

    def make_share(off):
        d = lax.rem(b + off, nb)
        total = jnp.zeros((radiance, PIX), jnp.float32)
        for k in range(nblocks):
            total = total + cover[k, d] * zbuf[:, k * PIX : (k + 1) * PIX].astype(jnp.float32)
        share[d] = total.astype(jnp.bfloat16)

    def send_share(off, carry):
        make_share(off)
        to_owner(off).start()
        return carry

    lax.fori_loop(1, nb, send_share, 0)
    make_share(0)

    fetches[0].wait()
    for a in range(3):
        for e, place in ((0, 2 - a), (2, 6 - a), (1, 8 + a)):
            kern_rows[place : place + 1, 0:channels] = kern[a, e : e + 1, :]
    taps[...] = kern_rows[...].T
    fetches[2].wait()
    wc[...] = wc_t[...].T

    lane = lax.broadcasted_iota(jnp.int32, (1, lon_cols), 1)

    at = {}
    for a in range(3):
        at[a, 0], at[a, 2], at[a, 1] = 2 - a, 6 - a, 8 + a

    def taps_of(targets):
        def body(c0, n):
            x = [rows[i, pl.ds(c0, n), :].astype(jnp.float32) for i in range(2)]
            tap = taps[pl.ds(c0, n), :]
            for t in targets:
                parts = []
                for e in range(3):
                    total = None
                    for i in range(2):
                        a = i - (t - 1) + 1
                        if 0 <= a < 3:
                            term = tap[:, at[a, e] : at[a, e] + 1] * x[i]
                            total = term if total is None else total + term
                    parts.append(total)
                west = jnp.where(lane == 0, 0.0, pltpu.roll(parts[0], 1, 1))
                east = jnp.where(lane == lon_cols - 1, 0.0, pltpu.roll(parts[2], lon_cols - 1, 1))
                mix[t, pl.ds(c0, n), :] = (parts[1] + west + east).astype(jnp.bfloat16)

        return body

    chunks(taps_of((0, 3)), 16)

    def to_neighbour(which):
        return pltpu.make_async_remote_copy(
            src_ref=psend.at[which],
            dst_ref=precv.at[which],
            send_sem=p_send.at[which],
            recv_sem=p_recv.at[which],
            device_id=(b - 1 if which == 0 else b + 1, l),
            device_id_type=MESH,
        )

    reaches = (b > 0, b < nb - 1)
    for which in range(2):
        psend[which] = dot(wc[...], mix[3 * which]).astype(jnp.bfloat16)

        @pl.when(reaches[which])
        def _():
            to_neighbour(which).start()

    elane = lax.broadcasted_iota(jnp.int32, (1, PIX), 1)
    ends = []
    for i in range(2):
        initial = rows[i, :, 0:PIX].astype(jnp.float32)[:, 0:1]
        last = rows[i, :, lon_cols - PIX : lon_cols].astype(jnp.float32)[:, PIX - 1 : PIX]
        ends.append(jnp.where(elane < 4, last, initial))
    edge0 = jnp.where(elane < 8, taps[0:channels, :], 0.0)
    edge = (ends[0] * edge0 + ends[1] * pltpu.roll(edge0, 1, 1)).astype(jnp.bfloat16)
    esend[...] = dot(edge, wc_t[...], 0, 0)[0:SLOTS].astype(jnp.bfloat16)

    def to_edge(m):
        db, dl = EDGES[m]
        return pltpu.make_async_remote_copy(
            src_ref=esend,
            dst_ref=erecv.at[pl.ds(m * SLOTS, SLOTS)],
            send_sem=e_send.at[m],
            recv_sem=e_recv.at[m],
            device_id=(b - db, lax.rem(l - dl + nl, nl)),
            device_id_type=MESH,
        )

    for m, (db, dl) in enumerate(EDGES):

        @pl.when((b - db >= 0) & (b - db < nb))
        def _():
            to_edge(m).start()

    def take_share(off, total):
        to_owner(off).wait_recv()
        return total + arrived[off].astype(jnp.float32)

    for i in range(7, 14):
        fetches[i].wait()
    evolved = lax.fori_loop(1, nb, take_share, share[b].astype(jnp.float32))
    departure = jnp.where(valid[...] == 1, evolved - observed[...], 0.0).astype(jnp.bfloat16)
    pre_dual = dot(res_t[...], departure, 0, 0) + dot(prev_t[...], dual_in[...], 0, 0)
    dual_hidden = jax.nn.gelu(
        pre_dual + jnp.broadcast_to(dual_bias[...], (PIX, dual_bias.shape[1])).T
    ).astype(jnp.bfloat16)
    updated = dual_in[...].astype(jnp.float32) + dot(dual_out_w[...], dual_hidden)
    gathered[0] = updated.astype(jnp.bfloat16)
    dual_new[...] = updated.astype(jnp.bfloat16)

    def to_all(off):
        return pltpu.make_async_remote_copy(
            src_ref=gathered.at[0],
            dst_ref=gathered.at[off],
            send_sem=g_send.at[off],
            recv_sem=g_recv.at[off],
            device_id=(lax.rem(b + off, nb), l),
            device_id_type=MESH,
        )

    def send_dual(off, carry):
        to_all(off).start()
        return carry

    lax.fori_loop(1, nb, send_dual, 0)

    fetches[3].wait()
    through_t[...] = dot(obs_op[...], wa_t[...]).astype(jnp.bfloat16)
    fetches[1].wait()
    ws[...] = ws_t[...].T
    chunks(taps_of((1, 2)), 16)
    fetches[4].wait()
    bias_wide = jnp.broadcast_to(bias[...], (PIX, hidden)).T
    for i in range(2):
        part = dot(ws[...], rows[i]) + dot(wc[...], mix[1 + i])
        for q in range(per_row):
            pre[i, :, q * PIX : (q + 1) * PIX] = part[:, q * PIX : (q + 1) * PIX] + bias_wide

    for m, (db, dl) in enumerate(EDGES):

        @pl.when((b + db >= 0) & (b + db < nb))
        def _():
            to_edge(m).wait_recv()

    pick = picker((len(EDGES) * SLOTS, 4 * PIX))
    fix = dot(erecv[...], pick, 0, 0)
    for i in range(2):
        pre[i, :, 0:PIX] = pre[i, :, 0:PIX] + fix[:, 2 * i * PIX : (2 * i + 1) * PIX]
        pre[i, :, lon_cols - PIX :] = (
            pre[i, :, lon_cols - PIX :] + fix[:, (2 * i + 1) * PIX : (2 * i + 2) * PIX]
        )

    def landed(off, carry):
        to_all(off).wait_recv()
        return carry

    lax.fori_loop(1, nb, landed, 0)
    for r in range(0, radiance, 16):

        def gather_in(off, totals):
            d = lax.rem(b - off + nb, nb)
            block = gathered[off, r : r + 16, :].astype(jnp.float32)
            return tuple(totals[k] + cover[k, d] * block for k in range(nblocks))

        zero = jnp.zeros((16, PIX), jnp.float32)
        totals = lax.fori_loop(0, nb, gather_in, (zero,) * nblocks, unroll=nb <= 8)
        for k in range(nblocks):
            back[r : r + 16, k * PIX : (k + 1) * PIX] = totals[k].astype(jnp.bfloat16)

    through = through_t[...].T
    for i in range(2):
        pre[i] = pre[i] + dot(through, back[:, i * lon_cols : (i + 1) * lon_cols])
    fetches[5].wait()
    for i in range(2):
        came = 1 - i

        @pl.when(reaches[i])
        def _():
            to_neighbour(came).wait_recv()

        for q in range(per_row):
            cols = slice(q * PIX, (q + 1) * PIX)
            hid[:, cols] = jax.nn.gelu(
                pre[i, :, cols] + precv[came, :, cols].astype(jnp.float32)
            ).astype(jnp.bfloat16)
        for q in range(0, per_row, 2):
            added = dot(w_out[...], hid[:, q * PIX : (q + 2) * PIX])
            place = pl.ds(i, channels, 2)
            for h in range(2):
                wide[q + h, place, :] = (
                    wide[q + h, place, :] + added[:, h * PIX : (h + 1) * PIX]
                )

    def pack(c0, n):
        for q in range(per_row):
            xb[pl.ds(2 * c0, 2 * n), q * PIX : (q + 1) * PIX] = wide[
                q, pl.ds(2 * c0, 2 * n), :
            ].astype(jnp.bfloat16)

    chunks(pack)
    store = pltpu.make_async_copy(xb, out.reshape(2 * channels, lon_cols), load_sem.at[0])
    store.start()

    def sent(off, carry):
        to_owner(off).wait_send()
        to_all(off).wait_send()
        return carry

    lax.fori_loop(1, nb, sent, 0)
    for which in range(2):

        @pl.when(reaches[which])
        def _():
            to_neighbour(which).wait_send()

    for m, (db, dl) in enumerate(EDGES):

        @pl.when((b - db >= 0) & (b - db < nb))
        def _():
            to_edge(m).wait_send()

    store.wait()


def on_device(
    state,
    kernel,
    w_state,
    w_conv,
    w_adj,
    bias_in,
    w_out,
    obs_op,
    observations,
    obs_mask,
    dual_in,
    dual_res,
    dual_prev,
    dual_bias,
    dual_out_w,
    footprint,
):
    channels, lat_rows, lon_cols = state.shape
    assert lat_rows == 2
    radiance = obs_op.shape[0]
    hidden = w_state.shape[0]
    nb = lax.axis_size("band")
    nblocks = lat_rows * lon_cols // PIX
    routes = footprint.reshape(nblocks, footprint.shape[-1]).T
    vmem = pl.BlockSpec(memory_space=pltpu.VMEM)
    anywhere = pl.BlockSpec(memory_space=pltpu.HBM)
    hbm = pl.BlockSpec(memory_space=pltpu.HBM)
    smem = pl.BlockSpec(memory_space=pltpu.SMEM)
    dma = pltpu.SemaphoreType.DMA
    bf16, f32 = jnp.bfloat16, jnp.float32
    held = (
        kernel.transpose(1, 2, 0),
        w_state.T,
        w_conv.T,
        w_adj.T,
        bias_in[None, :],
        w_out,
        obs_op,
        observations.reshape(radiance, PIX),
        obs_mask.reshape(radiance, PIX),
        dual_in.reshape(radiance, PIX),
        dual_res.T,
        dual_prev.T,
        dual_bias[None, :],
        dual_out_w,
    )
    padded = -(-channels // PIX) * PIX
    state_out, dual_new = pl.pallas_call(
        kernel_body,
        out_shape=(
            jax.ShapeDtypeStruct(state.shape, bf16),
            jax.ShapeDtypeStruct((radiance, PIX), bf16),
        ),
        in_specs=[anywhere] + [hbm] * len(held) + [smem],
        out_specs=(anywhere, vmem),
        scratch_shapes=[pltpu.VMEM(x.shape, x.dtype) for x in held]
        + [
            pltpu.SMEM((nblocks, nb), f32),
            pltpu.VMEM((PIX, padded), f32),
            pltpu.VMEM((padded, PIX), f32),
            pltpu.VMEM((hidden, channels), bf16),
            pltpu.VMEM((hidden, channels), bf16),
            pltpu.VMEM((2 * channels, lon_cols), bf16),
            pltpu.VMEM((lon_cols // PIX, 2 * channels, PIX), f32),
            pltpu.VMEM((2, channels, lon_cols), bf16),
            pltpu.VMEM((4, channels, lon_cols), bf16),
            pltpu.VMEM((2, hidden, lon_cols), f32),
            pltpu.VMEM((radiance, nblocks * PIX), bf16),
            pltpu.VMEM((nb, radiance, PIX), bf16),
            pltpu.VMEM((nb, radiance, PIX), bf16),
            pltpu.VMEM((nb, radiance, PIX), bf16),
            pltpu.VMEM((radiance, nblocks * PIX), bf16),
            pltpu.VMEM((radiance, hidden), bf16),
            pltpu.VMEM((hidden, lon_cols), bf16),
            pltpu.VMEM((2, hidden, lon_cols), bf16),
            pltpu.VMEM((2, hidden, lon_cols), bf16),
            pltpu.VMEM((SLOTS, hidden), bf16),
            pltpu.VMEM((len(EDGES) * SLOTS, hidden), bf16),
            dma((1,)),
            dma((len(held),)),
            dma((nb,)),
            dma((nb,)),
            dma((nb,)),
            dma((nb,)),
            dma((2,)),
            dma((2,)),
            dma((len(EDGES),)),
            dma((len(EDGES),)),
        ],
        compiler_params=pltpu.CompilerParams(
            collective_id=0, has_side_effects=True, vmem_limit_bytes=63 << 20
        ),
    )(state, *held, routes)
    return (state_out, dual_new.reshape(radiance, 1, PIX))


def solution(mesh):
    in_specs = (
        P(None, "band", "lon"),
        P(),
        P(),
        P(),
        P(),
        P(),
        P(),
        P(),
        P(None, "band", "lon"),
        P(None, "band", "lon"),
        P(None, "band", "lon"),
        P(),
        P(),
        P(),
        P(),
        P("band", "lon", None, None),
    )
    out_specs = (P(None, "band", "lon"), P(None, "band", "lon"))
    return jax.shard_map(
        on_device, mesh=mesh, in_specs=in_specs, out_specs=out_specs, check_vma=False
    )
```
